256 devices in a mesh: dp: 16 (over y_lo, z), section: 16 (over y_hi, x, core).
Axes of the slice: x: 4, y: 4 (y_hi: 2, y_lo: 2; y = y_hi * 2 + y_lo), z: 8, core: 2. Of those that a mesh axis runs over, the one named last changes fastest.
Arguments:
- section_inputs: bfloat16 [16, 4096, 2048], P('section', 'dp'), may hold values from -160 to 160
- enc_output: bfloat16 [4096, 2048], P('dp'), may hold values from -160 to 160
- attention_probs: bfloat16 [16, 128, 8, 32, 32], P('section', 'dp'), may hold values from 0 to 1, as said below
- value_weight: bfloat16 [16, 2048, 1024], P('section', 'dp'), may hold values from -0.125 to 0.125
- out_weight: bfloat16 [16, 1024, 2048], P('section', None, 'dp'), may hold values from -0.1875 to 0.1875
- norm_gain: float32 [16, 2048], P('section'), may hold values from 0.1 to 1.9
- top_grad: bfloat16 [4096, 2048], P('dp'), may hold values from -6 to 6
- enc_sentinel: int32 [128, 32], P('dp'), may hold values from 0 to 100, as said below
- dec_sentinel: int32 [128, 32], P('dp'), may hold values from 0 to 100, as said below
Outputs:
- section_input_grad: bfloat16 [16, 4096, 2048], P('section', 'dp')
- score_grad: bfloat16 [16, 128, 8, 32, 32], P('section', 'dp')
- value_weight_grad: bfloat16 [16, 2048, 1024], P('section', 'dp')
- out_weight_grad: bfloat16 [16, 1024, 2048], P('section', None, 'dp')
- gain_grad: float32 [16, 2048], P('section', 'dp')
- sentinel_grad: float32 [100, 2048], P(None, ('dp', 'section'))
The draws below stay inside these ranges and needn't reach their ends.
Inputs may be any that keep to these rules, and one draw needn't show every extreme that they name: `enc_sentinel`: along each sequence the positions that hold a sentinel carry the numbers 0, 1, 2, ... in order; the first position holds sentinel 0; 100 marks a position without a sentinel. `dec_sentinel`: along each sequence the positions that hold a sentinel carry the numbers 0, 1, 2, ... in order; the first position holds sentinel 0; 100 marks a position without a sentinel. `attention_probs`: each row over keys is a probability distribution, up to rounding.
All inputs are finite; a program needn't handle non-finite values.
Results may differ from the reference program's by a relative error of at most 0.027.
Values may be sent and summed in bfloat16 or wider, within the bound.
No kernel may reach another device: no remote copies, remote signals or barrier semaphores. Data moves between devices by JAX's collectives and lax.ppermute only.
A program may use at most 64 MiB of HBM per device.

```python
import math
import jax
import jax.numpy as jnp
from jax import lax

D = 2048
HEADS = 8
HDIM = 128
SENT = 100
LEN = 32
MICRO = 8
INNER = 1024
SEQS = 128
ROWS = 4096
SECTIONS = 16
N_DP = 16
N_SECTION = 16


def scaled_field(key, base_draw, row_low, row_high, column_low, column_high):
    row_key, column_key = jax.random.split(key, 2)
    row_scale = jnp.exp(jax.random.uniform(row_key, base_draw.shape[:-1] + (1,), jnp.float32, math.log(row_low), math.log(row_high)))
    column_scale = jnp.exp(jax.random.uniform(column_key, (base_draw.shape[-1],), jnp.float32, math.log(column_low), math.log(column_high)))
    blended = base_draw
    return blended * column_scale * row_scale


def draw_section_inputs(key, part):
    key = jax.random.fold_in(key, 11)
    base_key, scale_key = jax.random.split(key)
    array_shape = (SECTIONS, ROWS, D)
    base_draw = jnp.clip(jax.random.normal(base_key, array_shape, jnp.float32), -5.0, 5.0)
    return scaled_field(scale_key, base_draw, 1.0, 10.0, 0.3, 3.0).astype(jnp.bfloat16)


def draw_enc_output(key, part):
    key = jax.random.fold_in(key, 17)
    base_key, scale_key = jax.random.split(key)
    array_shape = (ROWS, D)
    base_draw = jnp.clip(jax.random.normal(base_key, array_shape, jnp.float32), -5.0, 5.0)
    return scaled_field(scale_key, base_draw, 0.5, 5.0, 0.3, 3.0).astype(jnp.bfloat16)


def draw_attention_probs(key, part):
    key = jax.random.fold_in(key, 23)
    array_shape = (SECTIONS, SEQS, HEADS, LEN, LEN)
    logits = 1.5 * jnp.clip(jax.random.normal(key, array_shape, jnp.float32), -5.0, 5.0)
    weights = jnp.exp(logits)
    return (weights / jnp.sum(weights, axis=-1, keepdims=True)).astype(jnp.bfloat16)


def span_numbers(key):
    density_key, mark_key = jax.random.split(key)
    density = jax.random.randint(density_key, (SEQS, 1), 2, 17)
    marked = (jax.random.randint(mark_key, (SEQS, LEN), 0, 16) < density).astype(jnp.int32)
    marked = marked.at[:, 0].set(1)
    running_count = jnp.cumsum(marked, axis=1) - 1
    keep_mark = jnp.logical_and(marked == 1, running_count < SENT)
    return jnp.where(keep_mark, running_count, SENT).astype(jnp.int32)


def draw_enc_sentinel(key, part):
    key = jax.random.fold_in(key, 31)
    return span_numbers(key)


def draw_dec_sentinel(key, part):
    key = jax.random.fold_in(key, 37)
    return span_numbers(key)


def steps_of(stream_key, extent, cuts, least, top_value):
    factor_of = 1.0
    for dim, parts in cuts:
        draws = jax.random.uniform(jax.random.fold_in(jax.random.fold_in(stream_key, 6), dim), (parts,), jnp.float32, least / len(cuts), top_value / len(cuts))
        factor_of = factor_of * jnp.repeat(jnp.exp(draws), extent[dim] // parts).reshape((-1,) + (1,) * (len(extent) - 1 - dim))
    return factor_of


def gaussian(own_key, extent, spread, most, pieces=(), kind=jnp.bfloat16):
    result = jax.random.normal(own_key, extent, jnp.float32) * spread
    if len(pieces) > 0:
        result = steps_of(own_key, extent, pieces, -0.22, 0.18) * result
    return jnp.clip(result, min=-most, max=most).astype(kind)


def setup_inputs(seed: int = 0) -> dict:
    keys = jax.random.split(jax.random.key(seed), 10)
    return {
        "section_inputs": draw_section_inputs(jax.random.fold_in(keys[9], 71), 0),
        "enc_output": draw_enc_output(jax.random.fold_in(keys[9], 71), 0),
        "attention_probs": draw_attention_probs(jax.random.fold_in(keys[9], 71), 0),
        "value_weight": gaussian(keys[3], (SECTIONS, D, INNER), D ** -0.5, 0.125, ((0, 16), (1, 16))),
        "out_weight": gaussian(keys[4], (SECTIONS, INNER, D), INNER ** -0.5, 0.1875, ((0, 16), (2, 16))),
        "norm_gain": jnp.clip(1.0 + 0.18 * jax.random.normal(keys[5], (SECTIONS, D), jnp.float32), 0.1, 1.9),
        "top_grad": gaussian(keys[6], (ROWS, D), 1.0, 6.0, ((0, 16),)),
        "enc_sentinel": draw_enc_sentinel(jax.random.fold_in(keys[9], 71), 0),
        "dec_sentinel": draw_dec_sentinel(jax.random.fold_in(keys[9], 71), 0),
    }


epsilon = 1e-06

def backward_block(out_grad, source, probs, gain_row, w_value, w_out):
    seq_total = source.shape[0]
    widened = source.astype(jnp.float32)
    inverse = lax.rsqrt(lax.optimization_barrier(jnp.mean(widened * widened, axis=-1, keepdims=True)) + epsilon)
    unit_rows = widened * inverse
    normed = (unit_rows * gain_row).astype(jnp.bfloat16)
    values = jnp.dot(normed.reshape(-1, D), w_value, preferred_element_type=jnp.float32).astype(jnp.bfloat16)
    head_values = values.reshape(seq_total, LEN, HEADS, HDIM).astype(jnp.float32)
    prob_wide = probs.astype(jnp.float32)
    context = jnp.einsum('bhqk,bkhd->bqhd', prob_wide, head_values).astype(jnp.bfloat16).reshape(-1, INNER)
    ctx_grad = jnp.dot(out_grad.reshape(-1, D), w_out.T, preferred_element_type=jnp.float32).astype(jnp.bfloat16)
    head_grads = ctx_grad.reshape(seq_total, LEN, HEADS, HDIM).astype(jnp.float32)
    prob_grad = jnp.einsum('bqhd,bkhd->bhqk', head_grads, head_values)
    score_grad = (prob_wide * (prob_grad - lax.optimization_barrier(jnp.sum(prob_grad * prob_wide, axis=-1, keepdims=True)))).astype(jnp.bfloat16)
    value_grad = jnp.einsum('bhqk,bqhd->bkhd', prob_wide, head_grads).astype(jnp.bfloat16).reshape(-1, INNER)
    normed_grad = jnp.dot(value_grad, w_value.T, preferred_element_type=jnp.float32).reshape(seq_total, LEN, D)
    scaled = normed_grad * gain_row
    source_grad = inverse * (scaled - unit_rows * lax.optimization_barrier(jnp.mean(scaled * unit_rows, axis=-1, keepdims=True)))
    gain_rows = normed_grad * unit_rows
    return (normed.reshape(-1, D), context, value_grad, score_grad, source_grad, gain_rows)

def replica_sum(left_rows, right_rows):
    left_wide = left_rows.reshape(N_DP, -1, left_rows.shape[-1]).astype(jnp.float32)
    right_wide = right_rows.reshape(N_DP, -1, right_rows.shape[-1]).astype(jnp.float32)
    replica_parts = jnp.einsum('rtd,rti->rdi', left_wide, right_wide).astype(jnp.bfloat16)
    replica_parts = lax.optimization_barrier(replica_parts)
    return lax.optimization_barrier(jnp.sum(replica_parts.astype(jnp.float32), axis=0))

def sentinel_rows(sentinel_ids, grads):
    onehot_table = (sentinel_ids.reshape(1, -1) == jnp.arange(SENT, dtype=jnp.int32)[:, None]).astype(jnp.bfloat16)
    return jnp.dot(onehot_table, grads.reshape(-1, D), preferred_element_type=jnp.float32)

def reference(section_inputs, enc_output, attention_probs, value_weight, out_weight, norm_gain, top_grad, enc_sentinel, dec_sentinel):
    half_point = N_SECTION // 2
    seq_total = N_DP * MICRO
    encoded = enc_output.reshape(seq_total, LEN, D)
    out_grad = top_grad.reshape(seq_total, LEN, D)
    enc_total = jnp.zeros((seq_total, LEN, D), jnp.float32)
    in_grads = [None] * N_SECTION
    score_list = [None] * N_SECTION
    value_list = [None] * N_SECTION
    output_list = [None] * N_SECTION
    gain_list = [None] * N_SECTION
    for section_number in range(N_SECTION - 1, -1, -1):
        is_cross = section_number >= half_point and (section_number - half_point) % 2 == 1
        if section_number == half_point - 1:
            out_grad = enc_total.astype(jnp.bfloat16)
        source = encoded if is_cross else section_inputs[section_number].reshape(seq_total, LEN, D)
        normed, context, value_grad, score_grad, source_grad, gain_rows = backward_block(out_grad, source, attention_probs[section_number], norm_gain[section_number], value_weight[section_number], out_weight[section_number])
        if is_cross:
            enc_total = enc_total + source_grad
            in_grad = out_grad
        else:
            in_grad = (out_grad.astype(jnp.float32) + source_grad).astype(jnp.bfloat16)
        in_grads[section_number] = in_grad.reshape(-1, D)
        score_list[section_number] = score_grad
        value_list[section_number] = replica_sum(normed, value_grad).astype(jnp.bfloat16)
        output_list[section_number] = replica_sum(context, out_grad.reshape(-1, D)).astype(jnp.bfloat16)
        gain_parts = lax.optimization_barrier(jnp.sum(gain_rows.reshape(N_DP, -1, D), axis=1)).astype(jnp.bfloat16)
        gain_parts = lax.optimization_barrier(gain_parts)
        gain_list[section_number] = lax.optimization_barrier(jnp.sum(gain_parts.astype(jnp.float32), axis=0))
        out_grad = in_grad
    sentinel_grad = sentinel_rows(enc_sentinel, in_grads[0]) + sentinel_rows(dec_sentinel, in_grads[half_point])
    return (jnp.stack(in_grads), jnp.stack(score_list), jnp.stack(value_list), jnp.stack(output_list), jnp.stack(gain_list), sentinel_grad)
```

```python
import jax
import jax.numpy as jnp
from jax import lax
from jax.sharding import PartitionSpec as P

SENT = 100
GROUP = 2
EPSILON = 1e-06


def chain_pairs(count, half):
    down = [(s, s - 2) for s in range(half + 1, count)]
    return down + [(s, s - 1) for s in range(1, half)]


def relay_pairs(count, half):
    return [(s, s + 1) for s in range(half, count - 2, 2)]


def chain_lag(section, count, half):
    decoder = (count - 1 - section) // 2
    encoder = half // 2 + (half - 1 - section)
    return jnp.where(section >= half, decoder, encoder)


def body(
    section_inputs,
    enc_output,
    attention_probs,
    value_weight,
    out_weight,
    norm_gain,
    top_grad,
    enc_sentinel,
    dec_sentinel,
):
    count = lax.axis_size("section")
    dp_count = lax.axis_size("dp")
    half = count // 2
    section = lax.axis_index("section")
    in_decoder = section >= half
    is_cross = jnp.logical_and(in_decoder, (section - half) % 2 == 1)
    is_top = section >= count - 2
    gathered = lax.all_gather(
        jnp.concatenate([value_weight[0], out_weight[0].T], axis=1), "dp", axis=0, tiled=True
    )
    inner = value_weight.shape[2]
    w_value = gathered[:, :inner]
    w_out = gathered[:, inner:]
    gain_row = norm_gain[0]
    micro, length = enc_sentinel.shape
    width = section_inputs.shape[2]
    heads = attention_probs.shape[2]
    rows = micro * length
    slots = micro // GROUP
    block = GROUP * length

    source = jnp.where(is_cross, enc_output, section_inputs[0])
    widened = source.astype(jnp.float32)
    inverse = lax.rsqrt(jnp.mean(widened * widened, axis=-1, keepdims=True) + EPSILON)
    normed = (widened * inverse * gain_row).astype(jnp.bfloat16)
    values = jnp.dot(normed, w_value, preferred_element_type=jnp.float32).astype(jnp.bfloat16)
    probs = attention_probs[0]
    source_slots = source.reshape(slots, block, width)
    inverse_slots = inverse.reshape(slots, block, 1)
    probs_slots = probs.reshape(slots, GROUP, heads, length, length)
    top_slots = top_grad.reshape(slots, block, width)
    lag = chain_lag(section, count, half)

    def pick(table, slot):
        return lax.dynamic_index_in_dim(table, slot, 0, keepdims=False)

    in_store = jnp.zeros((slots + 1, block, width), jnp.bfloat16)
    out_store = jnp.zeros((slots + 1, block, width), jnp.bfloat16)
    ctx_store = jnp.zeros((slots + 1, block, inner), jnp.bfloat16)
    vgrad_store = jnp.zeros((slots + 1, block, inner), jnp.bfloat16)
    gain_total = jnp.zeros((width,), jnp.float32)
    zeros = jnp.zeros((block, width), jnp.bfloat16)
    send = zeros
    for step in range(slots + half // 2 + half - 1):
        raw = step - lag
        active = jnp.logical_and(raw >= 0, raw < slots)
        slot = jnp.clip(raw, 0, slots - 1)
        keep = jnp.where(active, slot, slots)
        if step > 0:
            arrived = lax.ppermute(send, "section", chain_pairs(count, half))
            relayed = lax.ppermute(arrived, "section", relay_pairs(count, half))
        else:
            arrived = zeros
            relayed = zeros
        out_grad = jnp.where(is_top, pick(top_slots, slot), jnp.where(is_cross, relayed, arrived))
        ctx_grad = lax.dot_general(
            out_grad, w_out, (((1,), (0,)), ((), ())), preferred_element_type=jnp.float32
        ).astype(jnp.bfloat16)
        value_grad = jnp.einsum(
            "bhqk,bqhd->bkhd",
            pick(probs_slots, slot),
            ctx_grad.reshape(GROUP, length, heads, -1),
            preferred_element_type=jnp.float32,
        )
        value_grad = value_grad.astype(jnp.bfloat16).reshape(block, inner)
        normed_grad = lax.dot_general(
            value_grad, w_value, (((1,), (1,)), ((), ())), preferred_element_type=jnp.float32
        )
        scale = pick(inverse_slots, slot)
        unit = pick(source_slots, slot).astype(jnp.float32) * scale
        scaled = normed_grad * gain_row
        source_grad = scale * (scaled - unit * jnp.mean(scaled * unit, axis=-1, keepdims=True))
        gain_total = gain_total + jnp.where(active, jnp.sum(normed_grad * unit, axis=0), 0.0)
        widened_out = out_grad.astype(jnp.float32)
        in_grad = jnp.where(is_cross, widened_out, widened_out + source_grad).astype(jnp.bfloat16)
        running = jnp.where(section == count - 1, 0.0, arrived.astype(jnp.float32)) + source_grad
        send = jnp.where(is_cross, running.astype(jnp.bfloat16), in_grad)

        def put(store, piece):
            return lax.dynamic_update_index_in_dim(store, piece, keep, 0)

        in_store = put(in_store, in_grad)
        out_store = put(out_store, out_grad)
        ctx_store = put(ctx_store, ctx_grad)
        vgrad_store = put(vgrad_store, value_grad)

    in_rows = in_store[:slots].reshape(rows, width)
    out_rows = out_store[:slots].reshape(rows, width)
    value_rows = vgrad_store[:slots].reshape(rows, inner)
    head_grads = ctx_store[:slots].reshape(micro, length, heads, -1)
    head_values = values.reshape(micro, length, heads, -1)
    context = jnp.einsum(
        "bhqk,bkhd->bqhd", probs, head_values, preferred_element_type=jnp.float32
    )
    context = context.astype(jnp.bfloat16).reshape(rows, inner)
    prob_grad = jnp.einsum(
        "bqhd,bkhd->bhqk", head_grads, head_values, preferred_element_type=jnp.float32
    )
    prob_wide = probs.astype(jnp.float32)
    score_grad = (
        prob_wide * (prob_grad - jnp.sum(prob_grad * prob_wide, axis=-1, keepdims=True))
    ).astype(jnp.bfloat16)
    chosen = jnp.where(
        section == 0, enc_sentinel, jnp.where(section == half, dec_sentinel, SENT)
    )
    table = (chosen.reshape(1, -1) == jnp.arange(SENT, dtype=jnp.int32)[:, None]).astype(
        jnp.bfloat16
    )
    sentinel_term = jnp.dot(table, in_rows, preferred_element_type=jnp.float32)
    small = jnp.concatenate([sentinel_term, gain_total[None], jnp.zeros((3, width))], axis=0)
    small_rows = small.shape[0]
    small = small.astype(jnp.bfloat16).reshape(small_rows, dp_count, -1).transpose(1, 0, 2)
    piece = width // dp_count
    small = small.reshape(dp_count, -1, inner)
    value_term = jnp.einsum("td,ti->di", normed, value_rows, preferred_element_type=jnp.float32)
    output_term = jnp.einsum("td,ti->di", out_rows, context, preferred_element_type=jnp.float32)
    payload = jnp.concatenate(
        [
            value_term.astype(jnp.bfloat16).reshape(dp_count, piece, inner),
            output_term.astype(jnp.bfloat16).reshape(dp_count, piece, inner),
            small,
            jnp.zeros((dp_count, -small.shape[1] % 16, inner), jnp.bfloat16),
        ],
        axis=1,
    )
    summed = lax.psum_scatter(payload, "dp", scatter_dimension=0, tiled=True)[0]
    small_sum = summed[2 * piece : 2 * piece + small.shape[1]].reshape(small_rows, piece)
    small_sum = small_sum.astype(jnp.float32)
    sentinel_grad = lax.psum_scatter(
        small_sum[:SENT], "section", scatter_dimension=1, tiled=True
    )
    return (
        in_rows[None],
        score_grad[None],
        summed[:piece][None],
        summed[piece : 2 * piece].T[None],
        small_sum[SENT][None],
        sentinel_grad,
    )


def solution(mesh):
    placed = (
        P("section", "dp", None),
        P("dp", None),
        P("section", "dp", None, None, None),
        P("section", "dp", None),
        P("section", None, "dp"),
        P("section", None),
        P("dp", None),
        P("dp", None),
        P("dp", None),
    )
    return jax.shard_map(
        body,
        mesh=mesh,
        in_specs=placed,
        out_specs=(
            P("section", "dp", None),
            P("section", "dp", None, None, None),
            P("section", "dp", None),
            P("section", None, "dp"),
            P("section", "dp"),
            P(None, ("dp", "section")),
        ),
        check_vma=False,
    )
```

```python
import functools

import jax
import jax.numpy as jnp
from jax import lax
from jax.experimental import pallas as pl
from jax.experimental.pallas import tpu as pltpu
from jax.sharding import PartitionSpec as P

SENT = 100
STREAMS = 2
TILES = 4
EPSILON = 1e-06


def layer_kernel(
    cross, start, active, *refs
):
    has_side = cross == "sided"
    grad_hbm, *refs = refs
    if has_side:
        side_hbm, *refs = refs
    (weights, probs_hbm, source_hbm, inverse_hbm, gain_hbm, _, _, _, _, _), refs = (
        refs[:10],
        refs[10:],
    )
    send_hbm, out_hbm, in_hbm, ctx_hbm, vgrad_hbm, term_hbm, *refs = refs
    grad, side, probs, source, inverse, gain, ctx, vgrad, term, scaled, unit, send, sem = refs
    rows, width = grad.shape
    inner = ctx.shape[1]
    heads = probs.shape[0]
    head = inner // heads
    wide, tall = inner // TILES, width // TILES
    span = pl.ds(start * rows, rows)

    @pl.when(active[0] == 1)
    def _():
        loads = [
            pltpu.make_async_copy(origin, target, sem.at[index])
            for index, (origin, target) in enumerate(
                [
                    (grad_hbm, grad),
                    (probs_hbm.at[start], probs),
                    (source_hbm.at[span], source),
                    (inverse_hbm.at[span], inverse),
                    (gain_hbm, gain),
                ]
                + ([(side_hbm, side)] if has_side else [])
            )
        ]
        for load in loads:
            load.start()
        loads[0].wait()
        loads[1].wait()
        stores = [pltpu.make_async_copy(grad, out_hbm.at[span], sem.at[6])]
        if cross:
            stores.append(pltpu.make_async_copy(grad, in_hbm.at[span], sem.at[7]))
        for store in stores:
            store.start()
        arrived = grad[...]
        for tile in range(TILES):
            columns = slice(tile * wide, (tile + 1) * wide)
            piece = jnp.dot(
                arrived, weights[:, columns], preferred_element_type=jnp.float32
            ).astype(jnp.bfloat16)
            ctx[:, columns] = piece
            for index in range(wide // head):
                first = tile * wide + index * head
                vgrad[:, first : first + head] = jnp.dot(
                    probs[first // head],
                    piece[:, index * head : (index + 1) * head],
                    preferred_element_type=jnp.float32,
                ).astype(jnp.bfloat16)
        kept = [
            pltpu.make_async_copy(ctx, ctx_hbm.at[span], sem.at[8]),
            pltpu.make_async_copy(vgrad, vgrad_hbm.at[span], sem.at[9]),
        ]
        for store in kept:
            store.start()
        for load in loads[2:]:
            load.wait()
        value_grad = vgrad[...]
        scale = inverse[...]
        total = jnp.zeros((rows, 1), jnp.float32)
        for tile in range(TILES):
            columns = slice(tile * tall, (tile + 1) * tall)
            normed_grad = lax.dot_general(
                value_grad,
                weights[columns, inner:],
                (((1,), (1,)), ((), ())),
                preferred_element_type=jnp.float32,
            )
            unit_piece = source[:, columns].astype(jnp.float32) * scale
            product = normed_grad * unit_piece
            gain_piece = gain[:, columns]
            term[:, columns] = jnp.sum(product, axis=0, keepdims=True)
            total = total + jnp.sum(product * gain_piece, axis=1, keepdims=True)
            scaled[:, columns] = normed_grad * gain_piece
            unit[:, columns] = unit_piece
        source_grad = scale * (scaled[...] - unit[...] * (total / width))
        if has_side:
            source_grad = side[...].astype(jnp.float32) + source_grad
        elif not cross:
            source_grad = grad[...].astype(jnp.float32) + source_grad
        send[...] = source_grad.astype(jnp.bfloat16)
        last = [
            pltpu.make_async_copy(send, send_hbm, sem.at[10]),
            pltpu.make_async_copy(term, term_hbm.at[start], sem.at[11]),
        ]
        if not cross:
            last.append(pltpu.make_async_copy(send, in_hbm.at[span], sem.at[7]))
        for store in last:
            store.start()
        for store in stores + kept + last:
            store.wait()


def run_layer(cross, start, active, grad, side, fixed, stores):
    rows, width = grad.shape
    heads, inner = fixed[1].shape[1], stores[2].shape[1]
    anywhere = pl.BlockSpec(memory_space=pl.ANY)
    moving = [grad] + ([side] if cross == "sided" else [])
    shape = jax.ShapeDtypeStruct
    first = 1 + len(moving) + len(fixed)
    narrow = pltpu.VMEM((rows, width), jnp.bfloat16)
    inside = pltpu.VMEM((rows, inner), jnp.bfloat16)
    wide = pltpu.VMEM((rows, width), jnp.float32)
    send, *stores = pl.pallas_call(
        functools.partial(layer_kernel, cross, start),
        out_shape=(shape((rows, width), jnp.bfloat16),)
        + tuple(shape(store.shape, store.dtype) for store in stores),
        in_specs=[pl.BlockSpec(memory_space=pltpu.SMEM)]
        + [anywhere] * len(moving)
        + [pl.BlockSpec(memory_space=pltpu.VMEM)]
        + [anywhere] * (len(fixed) - 1 + len(stores)),
        out_specs=(anywhere,) * (1 + len(stores)),
        input_output_aliases={first + index: 1 + index for index in range(len(stores))},
        scratch_shapes=[
            narrow,
            narrow,
            pltpu.VMEM((heads, rows, rows), jnp.bfloat16),
            narrow,
            pltpu.VMEM((rows, 1), jnp.float32),
            pltpu.VMEM((1, width), jnp.float32),
            inside,
            inside,
            pltpu.VMEM((1, width), jnp.float32),
            wide,
            wide,
            narrow,
            pltpu.SemaphoreType.DMA((12,)),
        ],
        compiler_params=pltpu.CompilerParams(vmem_limit_bytes=24 * 1024 * 1024),
    )(active, *moving, *fixed, *stores)
    return send, tuple(stores)


def body(
    section_inputs,
    enc_output,
    attention_probs,
    value_weight,
    out_weight,
    norm_gain,
    top_grad,
    enc_sentinel,
    dec_sentinel,
):
    count = lax.axis_size("section")
    dp_count = lax.axis_size("dp")
    half = count // 2
    section = lax.axis_index("section")
    in_decoder = section >= half
    is_cross = jnp.logical_and(in_decoder, (section - half) % 2 == 1)
    gathered = lax.all_gather(
        jnp.concatenate([out_weight[0].T, value_weight[0]], axis=1), "dp", axis=0, tiled=True
    )
    inner = value_weight.shape[2]
    w_value = gathered[:, inner:]
    gain_row = norm_gain[0]
    micro, length = enc_sentinel.shape
    width = section_inputs.shape[2]
    heads = attention_probs.shape[2]
    rows = micro * length
    group = micro // STREAMS
    block = group * length

    source = jnp.where(is_cross, enc_output, section_inputs[0])
    widened = source.astype(jnp.float32)
    inverse = lax.rsqrt(jnp.mean(widened * widened, axis=-1, keepdims=True) + EPSILON)
    normed = (widened * inverse * gain_row).astype(jnp.bfloat16)
    values = jnp.dot(normed, w_value, preferred_element_type=jnp.float32).astype(jnp.bfloat16)
    probs = attention_probs[0]
    blocks = probs.reshape(STREAMS, group, heads, length, length).transpose(0, 2, 1, 4, 3)
    spread = jnp.eye(group, dtype=probs.dtype)[None, None, :, None, :, None]
    diagonal = (blocks[:, :, :, :, None, :] * spread).reshape(STREAMS, heads, block, block)
    fixed = (gathered, diagonal, source, inverse, gain_row[None])
    stores = (
        jnp.zeros((rows, width), jnp.bfloat16),
        jnp.zeros((rows, width), jnp.bfloat16),
        jnp.zeros((rows, inner), jnp.bfloat16),
        jnp.zeros((rows, inner), jnp.bfloat16),
        jnp.zeros((STREAMS, 1, width), jnp.float32),
    )

    def run(number, cross, grads, sides, stores):
        active = (section == number).astype(jnp.int32).reshape(1)
        sends = []
        for start in range(STREAMS):
            send, stores = run_layer(
                cross, start, active, grads[start], sides[start], fixed, stores
            )
            sends.append(send)
        return sends, stores

    def move(blocks, origin, target):
        return [lax.ppermute(one, "section", [(origin, target)]) for one in blocks]

    tops = [top_grad[start * block : (start + 1) * block] for start in range(STREAMS)]
    none = [None] * STREAMS
    main, stores = run(count - 2, "", tops, none, stores)
    side, stores = run(count - 1, "open", tops, none, stores)
    for number in range(count - 4, half, -2):
        grads = move(main, number + 2, number)
        sides = move(side, number + 3, number + 1)
        relayed = move(grads, number, number + 1)
        main, stores = run(number, "", grads, none, stores)
        side, stores = run(number + 1, "sided", relayed, sides, stores)
    grads = move(main, half + 2, half + 1)
    sides = move(side, half + 3, half + 1)
    relayed = move(grads, half + 1, half)
    main, stores = run(half + 1, "sided", grads, sides, stores)
    _, stores = run(half, "", relayed, none, stores)
    origin = half + 1
    for number in range(half - 1, -1, -1):
        main, stores = run(number, "", move(main, origin, number), none, stores)
        origin = number
    out_rows, in_rows, ctx_rows, value_rows, terms = stores
    gain_total = jnp.sum(terms, axis=(0, 1))
    head_grads = ctx_rows.reshape(micro, length, heads, -1)
    head_values = values.reshape(micro, length, heads, -1)
    context = jnp.einsum(
        "bhqk,bkhd->bqhd", probs, head_values, preferred_element_type=jnp.float32
    )
    context = context.astype(jnp.bfloat16).reshape(rows, inner)
    prob_grad = jnp.einsum(
        "bqhd,bkhd->bhqk", head_grads, head_values, preferred_element_type=jnp.float32
    )
    prob_wide = probs.astype(jnp.float32)
    score_grad = (
        prob_wide * (prob_grad - jnp.sum(prob_grad * prob_wide, axis=-1, keepdims=True))
    ).astype(jnp.bfloat16)
    chosen = jnp.where(
        section == 0, enc_sentinel, jnp.where(section == half, dec_sentinel, SENT)
    )
    table = (chosen.reshape(1, -1) == jnp.arange(SENT, dtype=jnp.int32)[:, None]).astype(
        jnp.bfloat16
    )
    sentinel_term = jnp.dot(table, in_rows, preferred_element_type=jnp.float32)
    small = jnp.concatenate([sentinel_term, gain_total[None], jnp.zeros((3, width))], axis=0)
    small_rows = small.shape[0]
    small = small.astype(jnp.bfloat16).reshape(small_rows, dp_count, -1).transpose(1, 0, 2)
    piece = width // dp_count
    small = small.reshape(dp_count, -1, inner)
    value_term = jnp.einsum("td,ti->di", normed, value_rows, preferred_element_type=jnp.float32)
    output_term = jnp.einsum("td,ti->di", out_rows, context, preferred_element_type=jnp.float32)
    payload = jnp.concatenate(
        [
            value_term.astype(jnp.bfloat16).reshape(dp_count, piece, inner),
            output_term.astype(jnp.bfloat16).reshape(dp_count, piece, inner),
            small,
            jnp.zeros((dp_count, -small.shape[1] % 16, inner), jnp.bfloat16),
        ],
        axis=1,
    )
    summed = lax.psum_scatter(payload, "dp", scatter_dimension=0, tiled=True)[0]
    small_sum = summed[2 * piece : 2 * piece + small.shape[1]].reshape(small_rows, piece)
    small_sum = small_sum.astype(jnp.float32)
    parts = small_sum.T.reshape(count, -1, small_rows)
    parts = lax.all_to_all(parts, "section", 0, 0, tiled=True)
    sentinel_grad = (parts[0] + parts[half]).T[:SENT]
    return (
        in_rows[None],
        score_grad[None],
        summed[:piece][None],
        summed[piece : 2 * piece].T[None],
        small_sum[SENT][None],
        sentinel_grad,
    )


def solution(mesh):
    placed = (
        P("section", "dp", None),
        P("dp", None),
        P("section", "dp", None, None, None),
        P("section", "dp", None),
        P("section", None, "dp"),
        P("section", None),
        P("dp", None),
        P("dp", None),
        P("dp", None),
    )
    return jax.shard_map(
        body,
        mesh=mesh,
        in_specs=placed,
        out_specs=(
            P("section", "dp", None),
            P("section", "dp", None, None, None),
            P("section", "dp", None),
            P("section", None, "dp"),
            P("section", "dp"),
            P(None, ("dp", "section")),
        ),
        check_vma=False,
    )
```

```python
import functools

import jax
import jax.numpy as jnp
from jax import lax
from jax.experimental import pallas as pl
from jax.experimental.pallas import tpu as pltpu
from jax.sharding import PartitionSpec as P

SENT = 100
STREAMS = 2
TILES = 4
EPSILON = 1e-06


def layer_kernel(
    cross, start, active, *refs
):
    has_side = cross == "sided"
    grad, *refs = refs
    if has_side:
        side, *refs = refs
    (weights, probs_hbm, source_hbm, inverse_hbm, gain_hbm, _, _, _, _, _), refs = (
        refs[:10],
        refs[10:],
    )
    send, out_hbm, in_hbm, ctx_hbm, vgrad_hbm, term_hbm, *refs = refs
    probs, source, inverse, gain, ctx, vgrad, term, scaled, unit, sem = refs
    rows, width = grad.shape
    inner = ctx.shape[1]
    heads = probs.shape[0]
    head = inner // heads
    wide, tall = inner // TILES, width // TILES
    span = pl.ds(start * rows, rows)

    @pl.when(active[0] == 1)
    def _():
        loads = [
            pltpu.make_async_copy(origin, target, sem.at[index])
            for index, (origin, target) in enumerate(
                [
                    (probs_hbm.at[start], probs),
                    (source_hbm.at[span], source),
                    (inverse_hbm.at[span], inverse),
                    (gain_hbm, gain),
                ]
            )
        ]
        for load in loads:
            load.start()
        loads[0].wait()
        stores = [pltpu.make_async_copy(grad, out_hbm.at[span], sem.at[6])]
        if cross:
            stores.append(pltpu.make_async_copy(grad, in_hbm.at[span], sem.at[7]))
        for store in stores:
            store.start()
        arrived = grad[...]
        for tile in range(TILES):
            columns = slice(tile * wide, (tile + 1) * wide)
            piece = jnp.dot(
                arrived, weights[:, columns], preferred_element_type=jnp.float32
            ).astype(jnp.bfloat16)
            ctx[:, columns] = piece
            for index in range(wide // head):
                first = tile * wide + index * head
                vgrad[:, first : first + head] = jnp.dot(
                    probs[first // head],
                    piece[:, index * head : (index + 1) * head],
                    preferred_element_type=jnp.float32,
                ).astype(jnp.bfloat16)
        kept = [
            pltpu.make_async_copy(ctx, ctx_hbm.at[span], sem.at[8]),
            pltpu.make_async_copy(vgrad, vgrad_hbm.at[span], sem.at[9]),
        ]
        for store in kept:
            store.start()
        for load in loads[1:]:
            load.wait()
        value_grad = vgrad[...]
        scale = inverse[...]
        total = jnp.zeros((rows, 1), jnp.float32)
        for tile in range(TILES):
            columns = slice(tile * tall, (tile + 1) * tall)
            normed_grad = lax.dot_general(
                value_grad,
                weights[columns, inner:],
                (((1,), (1,)), ((), ())),
                preferred_element_type=jnp.float32,
            )
            unit_piece = source[:, columns].astype(jnp.float32) * scale
            product = normed_grad * unit_piece
            gain_piece = gain[:, columns]
            term[:, columns] = jnp.sum(product, axis=0, keepdims=True)
            total = total + jnp.sum(product * gain_piece, axis=1, keepdims=True)
            scaled[:, columns] = normed_grad * gain_piece
            unit[:, columns] = unit_piece
        source_grad = scale * (scaled[...] - unit[...] * (total / width))
        if has_side:
            source_grad = side[...].astype(jnp.float32) + source_grad
        elif not cross:
            source_grad = grad[...].astype(jnp.float32) + source_grad
        send[...] = source_grad.astype(jnp.bfloat16)
        last = [
            pltpu.make_async_copy(term, term_hbm.at[start], sem.at[11]),
        ]
        if not cross:
            last.append(pltpu.make_async_copy(send, in_hbm.at[span], sem.at[7]))
        for store in last:
            store.start()
        for store in stores + kept + last:
            store.wait()


def load_kernel(origin, target, sem):
    copy = pltpu.make_async_copy(origin, target, sem)
    copy.start()
    copy.wait()


def load(array):
    return pl.pallas_call(
        load_kernel,
        out_shape=pltpu.VMEM(array.shape, array.dtype),
        in_specs=[pl.BlockSpec(memory_space=pltpu.HBM)],
        out_specs=pl.BlockSpec(memory_space=pltpu.VMEM),
        scratch_shapes=[pltpu.SemaphoreType.DMA(())],
        compiler_params=pltpu.CompilerParams(vmem_limit_bytes=16 * 1024 * 1024),
    )(array)


def run_layer(cross, start, active, grad, side, fixed, stores):
    rows, width = grad.shape
    heads, inner = fixed[1].shape[1], stores[2].shape[1]
    far = pl.BlockSpec(memory_space=pltpu.HBM)
    near = pl.BlockSpec(memory_space=pltpu.VMEM)
    moving = [grad] + ([side] if cross == "sided" else [])
    shape = jax.ShapeDtypeStruct
    first = 1 + len(moving) + len(fixed)
    narrow = pltpu.VMEM((rows, width), jnp.bfloat16)
    inside = pltpu.VMEM((rows, inner), jnp.bfloat16)
    wide = pltpu.VMEM((rows, width), jnp.float32)
    send, *stores = pl.pallas_call(
        functools.partial(layer_kernel, cross, start),
        out_shape=(shape((rows, width), jnp.bfloat16),)
        + tuple(shape(store.shape, store.dtype) for store in stores),
        in_specs=[pl.BlockSpec(memory_space=pltpu.SMEM)]
        + [near] * (len(moving) + 1)
        + [far] * (len(fixed) - 1 + len(stores)),
        out_specs=(near,) + (far,) * len(stores),
        input_output_aliases={first + index: 1 + index for index in range(len(stores))},
        scratch_shapes=[
            pltpu.VMEM((heads, rows, rows), jnp.bfloat16),
            narrow,
            pltpu.VMEM((rows, 1), jnp.float32),
            pltpu.VMEM((1, width), jnp.float32),
            inside,
            inside,
            pltpu.VMEM((1, width), jnp.float32),
            wide,
            wide,
            pltpu.SemaphoreType.DMA((12,)),
        ],
        compiler_params=pltpu.CompilerParams(vmem_limit_bytes=24 * 1024 * 1024),
    )(active, *moving, *fixed, *stores)
    return send, tuple(stores)


def body(
    section_inputs,
    enc_output,
    attention_probs,
    value_weight,
    out_weight,
    norm_gain,
    top_grad,
    enc_sentinel,
    dec_sentinel,
):
    count = lax.axis_size("section")
    dp_count = lax.axis_size("dp")
    half = count // 2
    section = lax.axis_index("section")
    in_decoder = section >= half
    is_cross = jnp.logical_and(in_decoder, (section - half) % 2 == 1)
    gathered = lax.all_gather(
        jnp.concatenate([out_weight[0].T, value_weight[0]], axis=1), "dp", axis=0, tiled=True
    )
    inner = value_weight.shape[2]
    w_value = gathered[:, inner:]
    gain_row = norm_gain[0]
    micro, length = enc_sentinel.shape
    width = section_inputs.shape[2]
    heads = attention_probs.shape[2]
    rows = micro * length
    group = micro // STREAMS
    block = group * length

    source = jnp.where(is_cross, enc_output, section_inputs[0])
    widened = source.astype(jnp.float32)
    inverse = lax.rsqrt(jnp.mean(widened * widened, axis=-1, keepdims=True) + EPSILON)
    normed = (widened * inverse * gain_row).astype(jnp.bfloat16)
    values = jnp.dot(normed, w_value, preferred_element_type=jnp.float32).astype(jnp.bfloat16)
    probs = attention_probs[0]
    blocks = probs.reshape(STREAMS, group, heads, length, length).transpose(0, 2, 1, 4, 3)
    spread = jnp.eye(group, dtype=probs.dtype)[None, None, :, None, :, None]
    diagonal = (blocks[:, :, :, :, None, :] * spread).reshape(STREAMS, heads, block, block)
    fixed = (load(gathered), diagonal, source, inverse, gain_row[None])
    stores = (
        jnp.zeros((rows, width), jnp.bfloat16),
        jnp.zeros((rows, width), jnp.bfloat16),
        jnp.zeros((rows, inner), jnp.bfloat16),
        jnp.zeros((rows, inner), jnp.bfloat16),
        jnp.zeros((STREAMS, 1, width), jnp.float32),
    )

    def run(number, cross, start, grad, side, stores):
        active = (section == number).astype(jnp.int32).reshape(1)
        return run_layer(cross, start, active, grad, side, fixed, stores)

    def move(one, origin, target):
        return lax.ppermute(one, "section", [(origin, target)])

    def after(one, other):
        return lax.optimization_barrier((one, other))[0]

    tops = [top_grad[start * block : (start + 1) * block] for start in range(STREAMS)]
    main, side = [None] * STREAMS, [None] * STREAMS
    for start in range(STREAMS):
        main[start], stores = run(count - 2, "", start, tops[start], None, stores)
    for start in range(STREAMS):
        side[start], stores = run(count - 1, "open", start, tops[start], None, stores)
    for number in range(count - 4, half, -2):
        relayed = [None] * STREAMS
        for start in range(STREAMS):
            grad = move(main[start], number + 2, number)
            if start:
                grad = after(grad, main[start - 1])
            relayed[start] = move(grad, number, number + 1)
            main[start], stores = run(number, "", start, grad, None, stores)
        for start in range(STREAMS):
            given = move(side[start], number + 3, number + 1)
            side[start], stores = run(
                number + 1, "sided", start, relayed[start], given, stores
            )
    grads = [None] * STREAMS
    for start in range(STREAMS):
        grad = move(main[start], half + 2, half + 1)
        given = move(side[start], half + 3, half + 1)
        if start:
            grad = after(grad, main[start - 1])
        main[start], stores = run(half + 1, "sided", start, grad, given, stores)
        grads[start] = grad
    for start in range(STREAMS):
        relayed = move(after(grads[start], main[-1]), half + 1, half)
        _, stores = run(half, "", start, relayed, None, stores)
    origin = half + 1
    for number in range(half - 1, -1, -1):
        for start in range(STREAMS):
            grad = move(main[start], origin, number)
            if start:
                grad = after(grad, main[start - 1])
            main[start], stores = run(number, "", start, grad, None, stores)
        origin = number
    out_rows, in_rows, ctx_rows, value_rows, terms = stores
    gain_total = jnp.sum(terms, axis=(0, 1))
    head_grads = ctx_rows.reshape(micro, length, heads, -1)
    head_values = values.reshape(micro, length, heads, -1)
    context = jnp.einsum(
        "bhqk,bkhd->bqhd", probs, head_values, preferred_element_type=jnp.float32
    )
    context = context.astype(jnp.bfloat16).reshape(rows, inner)
    prob_grad = jnp.einsum(
        "bqhd,bkhd->bhqk", head_grads, head_values, preferred_element_type=jnp.float32
    )
    prob_wide = probs.astype(jnp.float32)
    score_grad = (
        prob_wide * (prob_grad - jnp.sum(prob_grad * prob_wide, axis=-1, keepdims=True))
    ).astype(jnp.bfloat16)
    chosen = jnp.where(
        section == 0, enc_sentinel, jnp.where(section == half, dec_sentinel, SENT)
    )
    table = (chosen.reshape(1, -1) == jnp.arange(SENT, dtype=jnp.int32)[:, None]).astype(
        jnp.bfloat16
    )
    sentinel_term = jnp.dot(table, in_rows, preferred_element_type=jnp.float32)
    small = jnp.concatenate([sentinel_term, gain_total[None], jnp.zeros((3, width))], axis=0)
    small_rows = small.shape[0]
    small = small.astype(jnp.bfloat16).reshape(small_rows, dp_count, -1).transpose(1, 0, 2)
    piece = width // dp_count
    small = small.reshape(dp_count, -1, inner)
    value_term = jnp.einsum("td,ti->di", normed, value_rows, preferred_element_type=jnp.float32)
    output_term = jnp.einsum("td,ti->di", out_rows, context, preferred_element_type=jnp.float32)
    payload = jnp.concatenate(
        [
            value_term.astype(jnp.bfloat16).reshape(dp_count, piece, inner),
            output_term.astype(jnp.bfloat16).reshape(dp_count, piece, inner),
            small,
            jnp.zeros((dp_count, -small.shape[1] % 16, inner), jnp.bfloat16),
        ],
        axis=1,
    )
    summed = lax.psum_scatter(payload, "dp", scatter_dimension=0, tiled=True)[0]
    small_sum = summed[2 * piece : 2 * piece + small.shape[1]].reshape(small_rows, piece)
    small_sum = small_sum.astype(jnp.float32)
    parts = small_sum.T.reshape(count, -1, small_rows)
    parts = lax.all_to_all(parts, "section", 0, 0, tiled=True)
    sentinel_grad = (parts[0] + parts[half]).T[:SENT]
    return (
        in_rows[None],
        score_grad[None],
        summed[:piece][None],
        summed[piece : 2 * piece].T[None],
        small_sum[SENT][None],
        sentinel_grad,
    )


def solution(mesh):
    placed = (
        P("section", "dp", None),
        P("dp", None),
        P("section", "dp", None, None, None),
        P("section", "dp", None),
        P("section", None, "dp"),
        P("section", None),
        P("dp", None),
        P("dp", None),
        P("dp", None),
    )
    return jax.shard_map(
        body,
        mesh=mesh,
        in_specs=placed,
        out_specs=(
            P("section", "dp", None),
            P("section", "dp", None, None, None),
            P("section", "dp", None),
            P("section", None, "dp"),
            P("section", "dp"),
            P(None, ("dp", "section")),
        ),
        check_vma=False,
    )
```

```python
import functools

import jax
import jax.numpy as jnp
from jax import lax
from jax.experimental import pallas as pl
from jax.experimental.pallas import tpu as pltpu
from jax.sharding import PartitionSpec as P

SENT = 100
STREAMS = 2
TILES = 4
PAIR = 2
EPSILON = 1e-06


def layer_kernel(
    cross, start, number, active, *refs
):
    has_side = cross == "sided"
    grad, *refs = refs
    if has_side:
        side, *refs = refs
    (weights, probs_hbm, source_hbm, inverse_hbm, gain_hbm, _, _, _, _, _), refs = (
        refs[:10],
        refs[10:],
    )
    send, out_hbm, in_hbm, ctx_hbm, vgrad_hbm, term_hbm, *refs = refs
    probs, source, inverse, gain, ctx, vgrad, term, scaled, unit, sem = refs
    rows, width = grad.shape
    inner = ctx.shape[1]
    heads = probs.shape[0]
    head = inner // heads
    wide, tall = inner // TILES, width // TILES
    span = pl.ds(start * rows, rows)

    if number == 1:

        @pl.when(active[number] == 2)
        def _():
            copy = pltpu.make_async_copy(out_hbm.at[span], send, sem.at[10])
            copy.start()
            copy.wait()

    @pl.when(active[number] == 1)
    def _():
        loads = [
            pltpu.make_async_copy(origin, target, sem.at[index])
            for index, (origin, target) in enumerate(
                [
                    (probs_hbm.at[start], probs),
                    (source_hbm.at[span], source),
                    (inverse_hbm.at[span], inverse),
                    (gain_hbm, gain),
                ]
            )
        ]
        for load in loads:
            load.start()
        loads[0].wait()
        stores = [pltpu.make_async_copy(grad, out_hbm.at[span], sem.at[6])]
        if cross:
            stores.append(pltpu.make_async_copy(grad, in_hbm.at[span], sem.at[7]))
        for store in stores:
            store.start()
        arrived = grad[...]
        for tile in range(TILES):
            columns = slice(tile * wide, (tile + 1) * wide)
            piece = jnp.dot(
                arrived, weights[:, columns], preferred_element_type=jnp.float32
            ).astype(jnp.bfloat16)
            ctx[:, columns] = piece
            for index in range(wide // head):
                first = tile * wide + index * head
                vgrad[:, first : first + head] = jnp.dot(
                    probs[first // head],
                    piece[:, index * head : (index + 1) * head],
                    preferred_element_type=jnp.float32,
                ).astype(jnp.bfloat16)
        kept = [
            pltpu.make_async_copy(ctx, ctx_hbm.at[span], sem.at[8]),
            pltpu.make_async_copy(vgrad, vgrad_hbm.at[span], sem.at[9]),
        ]
        for store in kept:
            store.start()
        for load in loads[1:]:
            load.wait()
        value_grad = vgrad[...]
        scale = inverse[...]
        total = jnp.zeros((rows, 1), jnp.float32)
        for tile in range(TILES):
            columns = slice(tile * tall, (tile + 1) * tall)
            normed_grad = lax.dot_general(
                value_grad,
                weights[columns, inner:],
                (((1,), (1,)), ((), ())),
                preferred_element_type=jnp.float32,
            )
            unit_piece = source[:, columns].astype(jnp.float32) * scale
            product = normed_grad * unit_piece
            gain_piece = gain[:, columns]
            term[:, columns] = jnp.sum(product, axis=0, keepdims=True)
            total = total + jnp.sum(product * gain_piece, axis=1, keepdims=True)
            scaled[:, columns] = normed_grad * gain_piece
            unit[:, columns] = unit_piece
        source_grad = scale * (scaled[...] - unit[...] * (total / width))
        if has_side:
            source_grad = side[...].astype(jnp.float32) + source_grad
        elif not cross:
            source_grad = grad[...].astype(jnp.float32) + source_grad
        send[...] = source_grad.astype(jnp.bfloat16)
        last = [
            pltpu.make_async_copy(term, term_hbm.at[start], sem.at[11]),
        ]
        if not cross:
            last.append(pltpu.make_async_copy(send, in_hbm.at[span], sem.at[7]))
        for store in last:
            store.start()
        for store in stores + kept + last:
            store.wait()


def run_layer(cross, start, number, active, grad, side, fixed, stores):
    rows, width = grad.shape
    heads, inner = fixed[1].shape[1], stores[2].shape[1]
    far = pl.BlockSpec(memory_space=pltpu.HBM)
    near = pl.BlockSpec(memory_space=pltpu.VMEM)
    moving = [grad] + ([side] if cross == "sided" else [])
    shape = jax.ShapeDtypeStruct
    first = 1 + len(moving) + len(fixed)
    narrow = pltpu.VMEM((rows, width), jnp.bfloat16)
    inside = pltpu.VMEM((rows, inner), jnp.bfloat16)
    wide = pltpu.VMEM((rows, width), jnp.float32)
    send, *stores = pl.pallas_call(
        functools.partial(layer_kernel, cross, start, number),
        out_shape=(shape((rows, width), jnp.bfloat16),)
        + tuple(shape(store.shape, store.dtype) for store in stores),
        in_specs=[pl.BlockSpec(memory_space=pltpu.SMEM)]
        + [near] * (len(moving) + 1)
        + [far] * (len(fixed) - 1 + len(stores)),
        out_specs=(near,) + (far,) * len(stores),
        input_output_aliases={first + index: 1 + index for index in range(len(stores))},
        scratch_shapes=[
            pltpu.VMEM((heads, rows, rows), jnp.bfloat16),
            narrow,
            pltpu.VMEM((rows, 1), jnp.float32),
            pltpu.VMEM((1, width), jnp.float32),
            inside,
            inside,
            pltpu.VMEM((1, width), jnp.float32),
            wide,
            wide,
            pltpu.SemaphoreType.DMA((12,)),
        ],
        compiler_params=pltpu.CompilerParams(vmem_limit_bytes=12 * 1024 * 1024),
    )(active, *moving, *fixed, *stores)
    return send, tuple(stores)


def terms_kernel(normed, value_rows, out_rows, context, payload):
    pieces, rows, _ = payload.shape
    piece = (rows - 16) // 2
    for index in range(pieces):
        columns = slice(index * piece, (index + 1) * piece)
        for first, left, right in ((0, normed, value_rows), (piece, out_rows, context)):
            payload[index, first : first + piece] = lax.dot_general(
                left[:, columns],
                right[...],
                (((0,), (0,)), ((), ())),
                preferred_element_type=jnp.float32,
            ).astype(payload.dtype)


def gradient_terms(normed, value_rows, out_rows, context, pieces):
    rows, width = normed.shape
    inner = context.shape[1]
    piece = width // pieces
    sliced = pl.BlockSpec((rows, PAIR * piece), lambda step: (0, step))
    whole = pl.BlockSpec((rows, inner), lambda step: (0, 0))
    return pl.pallas_call(
        terms_kernel,
        grid=(pieces // PAIR,),
        out_shape=jax.ShapeDtypeStruct((pieces, 2 * piece + 16, inner), jnp.bfloat16),
        in_specs=[sliced, whole, sliced, whole],
        out_specs=pl.BlockSpec((PAIR, 2 * piece + 16, inner), lambda step: (step, 0, 0)),
        compiler_params=pltpu.CompilerParams(vmem_limit_bytes=16 * 1024 * 1024),
    )(normed, value_rows, out_rows, context)


def body(
    section_inputs,
    enc_output,
    attention_probs,
    value_weight,
    out_weight,
    norm_gain,
    top_grad,
    enc_sentinel,
    dec_sentinel,
):
    count = lax.axis_size("section")
    dp_count = lax.axis_size("dp")
    half = count // 2
    section = lax.axis_index("section")
    in_decoder = section >= half
    is_cross = jnp.logical_and(in_decoder, (section - half) % 2 == 1)
    gathered = lax.all_gather(
        jnp.concatenate([out_weight[0].T, value_weight[0]], axis=1), "dp", axis=0, tiled=True
    )
    inner = value_weight.shape[2]
    w_value = gathered[:, inner:]
    gain_row = norm_gain[0]
    micro, length = enc_sentinel.shape
    width = section_inputs.shape[2]
    heads = attention_probs.shape[2]
    rows = micro * length
    group = micro // STREAMS
    block = group * length

    source = jnp.where(is_cross, enc_output, section_inputs[0])
    widened = source.astype(jnp.float32)
    inverse = lax.rsqrt(jnp.mean(widened * widened, axis=-1, keepdims=True) + EPSILON)
    normed = (widened * inverse * gain_row).astype(jnp.bfloat16)
    values = jnp.dot(normed, w_value, preferred_element_type=jnp.float32).astype(jnp.bfloat16)
    probs = attention_probs[0]
    blocks = probs.reshape(STREAMS, group, heads, length, length).transpose(0, 2, 1, 4, 3)
    spread = jnp.eye(group, dtype=probs.dtype)[None, None, :, None, :, None]
    diagonal = (blocks[:, :, :, :, None, :] * spread).reshape(STREAMS, heads, block, block)
    fixed = (gathered, diagonal, source, inverse, gain_row[None])
    stores = (
        jnp.zeros((rows, width), jnp.bfloat16),
        jnp.zeros((rows, width), jnp.bfloat16),
        jnp.zeros((rows, inner), jnp.bfloat16),
        jnp.zeros((rows, inner), jnp.bfloat16),
        jnp.zeros((STREAMS, 1, width), jnp.float32),
    )

    numbers = jnp.arange(count)
    active = jnp.where(section == numbers, 1, 0).astype(jnp.int32)
    active = jnp.where((section == half) & (numbers == 0), 1, active)
    active = jnp.where((section == half) & (numbers == half), 0, active)
    active = jnp.where((section == half + 1) & (numbers == 1), 2, active)

    def run(number, cross, start, grad, side, stores):
        with jax.named_scope(f"k{number}_{start}"):
            return run_layer(cross, start, number, active, grad, side, fixed, stores)

    def move(one, start, *pairs):
        with jax.named_scope(f"p{pairs[0][0]}_{pairs[0][1]}_{start}"):
            return lax.ppermute(one, "section", pairs)

    def after(one, other):
        return lax.optimization_barrier((one, other))[0]

    tops = [top_grad[start * block : (start + 1) * block] for start in range(STREAMS)]
    main, side = [None] * STREAMS, [None] * STREAMS
    for start in range(STREAMS):
        main[start], stores = run(count - 2, "", start, tops[start], None, stores)
    for start in range(STREAMS):
        side[start], stores = run(count - 1, "open", start, tops[start], None, stores)
    grads = [move(main[start], start, (count - 2, count - 4)) for start in range(STREAMS)]
    grads[0] = after(grads[0], main[-1])
    given = [move(side[start], start, (count - 1, count - 3)) for start in range(STREAMS)]
    for number in range(count - 4, half, -2):
        target = number - 2 if number - 2 > half else half + 1
        relayed, following, sending = ([None] * STREAMS for _ in range(3))
        for start in range(STREAMS):
            grad = grads[start]
            if start:
                grad = after(grad, main[start - 1])
            relayed[start] = move(grad, start, (number, number + 1))
            if not start:
                grad = after(grad, relayed[start])
            main[start], stores = run(number, "", start, grad, None, stores)
            following[start] = move(main[start], start, (number, target))
            one = relayed[start]
            if start and number > half + 2:
                one = after(one, sending[start - 1])
            side[start], stores = run(number + 1, "sided", start, one, given[start], stores)
            sending[start] = move(side[start], start, (number + 1, number - 1))
        grads, given = following, sending
        grads[0] = after(grads[0], main[-1])
    for number in [half + 1] + list(range(half - 1, -1, -1)):
        for start in range(STREAMS):
            if number == half - 1:
                pairs = [(half + 1, number)]
            elif number == 0:
                pairs = [(1, 0), (half + 1, half)]
            else:
                pairs = [(number + 1, number)]
            grad = grads[start] if number > half else move(main[start], start, *pairs)
            if start:
                grad = after(grad, main[start - 1])
            main[start], stores = run(
                number, "sided" if number > half else "", start, grad, given[start], stores
            )
    out_rows, in_rows, ctx_rows, value_rows, terms = stores
    gain_total = jnp.sum(terms, axis=(0, 1))
    head_grads = ctx_rows.reshape(micro, length, heads, -1)
    head_values = values.reshape(micro, length, heads, -1)
    context = jnp.einsum(
        "bhqk,bkhd->bqhd", probs, head_values, preferred_element_type=jnp.float32
    )
    context = context.astype(jnp.bfloat16).reshape(rows, inner)
    prob_grad = jnp.einsum(
        "bqhd,bkhd->bhqk", head_grads, head_values, preferred_element_type=jnp.float32
    )
    prob_wide = probs.astype(jnp.float32)
    score_grad = (
        prob_wide * (prob_grad - jnp.sum(prob_grad * prob_wide, axis=-1, keepdims=True))
    ).astype(jnp.bfloat16)
    piece = width // dp_count
    chosen = jnp.where(
        section == 0, enc_sentinel, jnp.where(section == half, dec_sentinel, SENT)
    )
    table = (chosen.reshape(1, -1) == jnp.arange(SENT, dtype=jnp.int32)[:, None]).astype(
        jnp.bfloat16
    )
    sentinel_term = jnp.dot(table, in_rows, preferred_element_type=jnp.float32)
    share = piece // count
    parts = sentinel_term.reshape(SENT, dp_count, count, share).transpose(2, 0, 1, 3)
    parts = parts.reshape(count, SENT, dp_count * share)
    parts = lax.all_to_all(parts, "section", 0, 0, tiled=True)
    payload = gradient_terms(normed, value_rows, out_rows, context, dp_count)
    parts = (parts[0] + parts[half]).reshape(SENT, dp_count, share).transpose(1, 0, 2)
    parts = jnp.concatenate(
        [parts.reshape(dp_count, -1), gain_total.reshape(dp_count, piece)], axis=1
    ).astype(jnp.bfloat16)
    parts = jnp.pad(parts, ((0, 0), (0, 16 * inner - parts.shape[1])))
    payload = lax.dynamic_update_slice(
        payload, parts.reshape(dp_count, 16, inner), (0, 2 * piece, 0)
    )
    summed = lax.psum_scatter(payload, "dp", scatter_dimension=0, tiled=True)[0]
    parts = summed[2 * piece].astype(jnp.float32)
    sentinel_grad = parts[: SENT * share].reshape(SENT, share)
    gain_sum = parts[SENT * share : SENT * share + piece]
    return (
        in_rows[None],
        score_grad[None],
        summed[:piece][None],
        summed[piece : 2 * piece].T[None],
        gain_sum[None],
        sentinel_grad,
    )


def solution(mesh):
    placed = (
        P("section", "dp", None),
        P("dp", None),
        P("section", "dp", None, None, None),
        P("section", "dp", None),
        P("section", None, "dp"),
        P("section", None),
        P("dp", None),
        P("dp", None),
        P("dp", None),
    )
    return jax.shard_map(
        body,
        mesh=mesh,
        in_specs=placed,
        out_specs=(
            P("section", "dp", None),
            P("section", "dp", None, None, None),
            P("section", "dp", None),
            P("section", None, "dp"),
            P("section", "dp"),
            P(None, ("dp", "section")),
        ),
        check_vma=False,
    )
```

```python
import functools

import jax
import jax.numpy as jnp
from jax import lax
from jax.experimental import pallas as pl
from jax.experimental.pallas import tpu as pltpu
from jax.sharding import PartitionSpec as P

SENT = 100
STREAMS = 2
TILES = 4
PAIR = 2
EPSILON = 1e-06


def layer_kernel(
    cross, start, number, active, *refs
):
    has_side = cross == "sided"
    grad, *refs = refs
    if has_side:
        side, *refs = refs
    (weights, probs_hbm, source_hbm, inverse_hbm, gain_hbm, _, _, _, _, _), refs = (
        refs[:10],
        refs[10:],
    )
    send, out_hbm, in_hbm, ctx_hbm, vgrad_hbm, term_hbm, *refs = refs
    probs, source, inverse, gain, ctx, vgrad, term, scaled, unit, sem = refs
    rows, width = grad.shape
    inner = ctx.shape[1]
    heads = probs.shape[0]
    head = inner // heads
    wide, tall = inner // TILES, width // TILES
    span = pl.ds(start * rows, rows)

    if number == 1:

        @pl.when(active[number] == 2)
        def _():
            copy = pltpu.make_async_copy(out_hbm.at[span], send, sem.at[10])
            copy.start()
            copy.wait()

    @pl.when(active[number] == 1)
    def _():
        loads = [
            pltpu.make_async_copy(origin, target, sem.at[index])
            for index, (origin, target) in enumerate(
                [
                    (probs_hbm.at[start], probs),
                    (source_hbm.at[span], source),
                    (inverse_hbm.at[span], inverse),
                    (gain_hbm, gain),
                ]
            )
        ]
        for load in loads:
            load.start()
        loads[0].wait()
        stores = [pltpu.make_async_copy(grad, out_hbm.at[span], sem.at[6])]
        if cross:
            stores.append(pltpu.make_async_copy(grad, in_hbm.at[span], sem.at[7]))
        for store in stores:
            store.start()
        arrived = grad[...]
        for tile in range(TILES):
            columns = slice(tile * wide, (tile + 1) * wide)
            piece = jnp.dot(
                arrived, weights[:, columns], preferred_element_type=jnp.float32
            ).astype(jnp.bfloat16)
            ctx[:, columns] = piece
            for index in range(wide // head):
                first = tile * wide + index * head
                vgrad[:, first : first + head] = jnp.dot(
                    probs[first // head],
                    piece[:, index * head : (index + 1) * head],
                    preferred_element_type=jnp.float32,
                ).astype(jnp.bfloat16)
        kept = [
            pltpu.make_async_copy(ctx, ctx_hbm.at[span], sem.at[8]),
            pltpu.make_async_copy(vgrad, vgrad_hbm.at[span], sem.at[9]),
        ]
        for store in kept:
            store.start()
        for load in loads[1:]:
            load.wait()
        value_grad = vgrad[...]
        scale = inverse[...]
        total = jnp.zeros((rows, 1), jnp.float32)
        for tile in range(TILES):
            columns = slice(tile * tall, (tile + 1) * tall)
            normed_grad = lax.dot_general(
                value_grad,
                weights[columns, inner:],
                (((1,), (1,)), ((), ())),
                preferred_element_type=jnp.float32,
            )
            unit_piece = source[:, columns].astype(jnp.float32) * scale
            product = normed_grad * unit_piece
            gain_piece = gain[:, columns]
            term[:, columns] = jnp.sum(product, axis=0, keepdims=True)
            total = total + jnp.sum(product * gain_piece, axis=1, keepdims=True)
            scaled[:, columns] = normed_grad * gain_piece
            unit[:, columns] = unit_piece
        source_grad = scale * (scaled[...] - unit[...] * (total / width))
        if has_side:
            source_grad = side[...].astype(jnp.float32) + source_grad
        elif not cross:
            source_grad = grad[...].astype(jnp.float32) + source_grad
        send[...] = source_grad.astype(jnp.bfloat16)
        last = [
            pltpu.make_async_copy(term, term_hbm.at[start], sem.at[11]),
        ]
        if not cross:
            last.append(pltpu.make_async_copy(send, in_hbm.at[span], sem.at[7]))
        for store in last:
            store.start()
        for store in stores + kept + last:
            store.wait()


def run_layer(cross, start, number, active, grad, side, fixed, stores):
    rows, width = grad.shape
    heads, inner = fixed[1].shape[1], stores[2].shape[1]
    far = pl.BlockSpec(memory_space=pltpu.HBM)
    near = pl.BlockSpec(memory_space=pltpu.VMEM)
    moving = [grad] + ([side] if cross == "sided" else [])
    shape = jax.ShapeDtypeStruct
    first = 1 + len(moving) + len(fixed)
    narrow = pltpu.VMEM((rows, width), jnp.bfloat16)
    inside = pltpu.VMEM((rows, inner), jnp.bfloat16)
    wide = pltpu.VMEM((rows, width), jnp.float32)
    send, *stores = pl.pallas_call(
        functools.partial(layer_kernel, cross, start, number),
        out_shape=(shape((rows, width), jnp.bfloat16),)
        + tuple(shape(store.shape, store.dtype) for store in stores),
        in_specs=[pl.BlockSpec(memory_space=pltpu.SMEM)]
        + [near] * (len(moving) + 1)
        + [far] * (len(fixed) - 1 + len(stores)),
        out_specs=(near,) + (far,) * len(stores),
        input_output_aliases={first + index: 1 + index for index in range(len(stores))},
        scratch_shapes=[
            pltpu.VMEM((heads, rows, rows), jnp.bfloat16),
            narrow,
            pltpu.VMEM((rows, 1), jnp.float32),
            pltpu.VMEM((1, width), jnp.float32),
            inside,
            inside,
            pltpu.VMEM((1, width), jnp.float32),
            wide,
            wide,
            pltpu.SemaphoreType.DMA((12,)),
        ],
        compiler_params=pltpu.CompilerParams(vmem_limit_bytes=20 * 1024 * 1024),
    )(active, *moving, *fixed, *stores)
    return send, tuple(stores)


def terms_kernel(normed, value_rows, out_rows, context, payload):
    pieces, rows, _ = payload.shape
    piece = rows // 2
    for index in range(pieces):
        columns = slice(index * piece, (index + 1) * piece)
        for first, left, right in ((0, normed, value_rows), (piece, out_rows, context)):
            payload[index, first : first + piece] = lax.dot_general(
                left[:, columns],
                right[...],
                (((0,), (0,)), ((), ())),
                preferred_element_type=jnp.float32,
            ).astype(payload.dtype)


def gradient_terms(normed, value_rows, out_rows, context, pieces):
    rows, width = normed.shape
    inner = context.shape[1]
    piece = width // pieces
    sliced = pl.BlockSpec((rows, PAIR * piece), lambda step: (0, step))
    whole = pl.BlockSpec((rows, inner), lambda step: (0, 0))
    return pl.pallas_call(
        terms_kernel,
        grid=(pieces // PAIR,),
        out_shape=pltpu.HBM((pieces, 2 * piece, inner), jnp.bfloat16),
        in_specs=[sliced, whole, sliced, whole],
        out_specs=pl.BlockSpec((PAIR, 2 * piece, inner), lambda step: (step, 0, 0)),
        compiler_params=pltpu.CompilerParams(vmem_limit_bytes=16 * 1024 * 1024),
    )(normed, value_rows, out_rows, context)


def body(
    section_inputs,
    enc_output,
    attention_probs,
    value_weight,
    out_weight,
    norm_gain,
    top_grad,
    enc_sentinel,
    dec_sentinel,
):
    count = lax.axis_size("section")
    dp_count = lax.axis_size("dp")
    half = count // 2
    section = lax.axis_index("section")
    in_decoder = section >= half
    is_cross = jnp.logical_and(in_decoder, (section - half) % 2 == 1)
    gathered = lax.all_gather(
        jnp.concatenate([out_weight[0].T, value_weight[0]], axis=1), "dp", axis=0, tiled=True
    )
    inner = value_weight.shape[2]
    w_value = gathered[:, inner:]
    gain_row = norm_gain[0]
    micro, length = enc_sentinel.shape
    width = section_inputs.shape[2]
    heads = attention_probs.shape[2]
    rows = micro * length
    group = micro // STREAMS
    block = group * length

    source = jnp.where(is_cross, enc_output, section_inputs[0])
    widened = source.astype(jnp.float32)
    inverse = lax.rsqrt(jnp.mean(widened * widened, axis=-1, keepdims=True) + EPSILON)
    normed = (widened * inverse * gain_row).astype(jnp.bfloat16)
    probs = attention_probs[0]
    blocks = probs.reshape(STREAMS, group, heads, length, length).transpose(0, 2, 1, 4, 3)
    spread = jnp.eye(group, dtype=probs.dtype)[None, None, :, None, :, None]
    diagonal = (blocks[:, :, :, :, None, :] * spread).reshape(STREAMS, heads, block, block)
    fixed = (gathered, diagonal, source, inverse, gain_row[None])
    stores = (
        jnp.zeros((rows, width), jnp.bfloat16),
        jnp.zeros((rows, width), jnp.bfloat16),
        jnp.zeros((rows, inner), jnp.bfloat16),
        jnp.zeros((rows, inner), jnp.bfloat16),
        jnp.zeros((STREAMS, 1, width), jnp.float32),
    )

    numbers = jnp.arange(count)
    active = jnp.where(section == numbers, 1, 0).astype(jnp.int32)
    active = jnp.where((section == half) & (numbers == 0), 1, active)
    active = jnp.where((section == half) & (numbers == half), 0, active)
    active = jnp.where((section == half + 1) & (numbers == 1), 2, active)

    def run(number, cross, start, grad, side, stores):
        with jax.named_scope(f"k{number}_{start}"):
            return run_layer(cross, start, number, active, grad, side, fixed, stores)

    def move(one, start, *pairs):
        with jax.named_scope(f"p{pairs[0][0]}_{pairs[0][1]}_{start}"):
            return lax.ppermute(one, "section", pairs)

    def after(one, other):
        return lax.optimization_barrier((one, other))[0]

    tops = [top_grad[start * block : (start + 1) * block] for start in range(STREAMS)]
    chosen = jnp.where(
        section == 0, enc_sentinel, jnp.where(section == half, dec_sentinel, SENT)
    )
    table = (chosen.reshape(1, -1) == jnp.arange(SENT, dtype=jnp.int32)[:, None]).astype(
        jnp.bfloat16
    )
    tops[0], table, active = lax.optimization_barrier((tops[0], table, active))
    main, side = [None] * STREAMS, [None] * STREAMS
    for start in range(STREAMS):
        main[start], stores = run(count - 2, "", start, tops[start], None, stores)
    for start in range(STREAMS):
        side[start], stores = run(count - 1, "open", start, tops[start], None, stores)
    grads = [move(main[start], start, (count - 2, count - 4)) for start in range(STREAMS)]
    grads[0] = after(grads[0], main[-1])
    given = [move(side[start], start, (count - 1, count - 3)) for start in range(STREAMS)]
    for number in range(count - 4, half, -2):
        target = number - 2 if number - 2 > half else half + 1
        relayed, following, sending = ([None] * STREAMS for _ in range(3))
        for start in range(STREAMS):
            grad = grads[start]
            if start:
                grad = after(grad, main[start - 1])
            relayed[start] = move(grad, start, (number, number + 1))
            if not start:
                grad = after(grad, relayed[start])
            main[start], stores = run(number, "", start, grad, None, stores)
            following[start] = move(main[start], start, (number, target))
            one = relayed[start]
            if start and number > half + 2:
                one = after(one, sending[start - 1])
            side[start], stores = run(number + 1, "sided", start, one, given[start], stores)
            sending[start] = move(side[start], start, (number + 1, number - 1))
        grads, given = following, sending
        grads[0] = after(grads[0], main[-1])
    for number in [half + 1] + list(range(half - 1, -1, -1)):
        if number == half - 1:
            values = jnp.dot(after(normed, main[-1]), w_value, preferred_element_type=jnp.float32).astype(jnp.bfloat16)
            head_values = values.reshape(micro, length, heads, -1)
            context = jnp.einsum(
                "bhqk,bkhd->bqhd", probs, head_values, preferred_element_type=jnp.float32
            )
            context = context.astype(jnp.bfloat16).reshape(rows, inner)
        for start in range(STREAMS):
            if number == half - 1:
                pairs = [(half + 1, number)]
            elif number == 0:
                pairs = [(1, 0), (half + 1, half)]
            else:
                pairs = [(number + 1, number)]
            grad = grads[start] if number > half else move(main[start], start, *pairs)
            if start:
                grad = after(grad, main[start - 1])
            elif number == half - 1:
                grad, context, values = lax.optimization_barrier((grad, context, values))
            main[start], stores = run(
                number, "sided" if number > half else "", start, grad, given[start], stores
            )
    out_rows, in_rows, ctx_rows, value_rows, terms = stores
    gain_total = jnp.sum(terms, axis=(0, 1))
    head_grads = ctx_rows.reshape(micro, length, heads, -1)
    prob_grad = jnp.einsum(
        "bqhd,bkhd->bhqk", head_grads, head_values, preferred_element_type=jnp.float32
    )
    prob_wide = probs.astype(jnp.float32)
    score_grad = (
        prob_wide * (prob_grad - jnp.sum(prob_grad * prob_wide, axis=-1, keepdims=True))
    ).astype(jnp.bfloat16)
    piece = width // dp_count
    sentinel_term = jnp.dot(table, in_rows, preferred_element_type=jnp.float32)
    share = piece // count
    parts = sentinel_term.reshape(SENT, dp_count, count, share).transpose(2, 0, 1, 3)
    parts = parts.reshape(count, SENT, dp_count * share)
    parts = lax.all_to_all(parts, "section", 0, 0, tiled=True)
    payload = gradient_terms(normed, value_rows, out_rows, context, dp_count)
    summed = lax.psum_scatter(payload, "dp", scatter_dimension=0, tiled=True)[0]
    parts = (parts[0] + parts[half]).reshape(SENT, dp_count, share).transpose(1, 0, 2)
    parts = jnp.concatenate(
        [parts.reshape(dp_count, -1), gain_total.reshape(dp_count, piece)], axis=1
    )
    parts = jnp.pad(parts, ((0, 0), (0, -parts.shape[1] % 1024)))
    parts = parts.reshape(dp_count, -1, 128)
    parts = jnp.sum(lax.all_to_all(parts, "dp", 0, 0, tiled=True), axis=0).reshape(-1)
    sentinel_grad = parts[: SENT * share].reshape(SENT, share)
    gain_sum = parts[SENT * share : SENT * share + piece]
    return (
        in_rows[None],
        score_grad[None],
        summed[:piece][None],
        summed[piece:].T[None],
        gain_sum[None],
        sentinel_grad,
    )


def solution(mesh):
    placed = (
        P("section", "dp", None),
        P("dp", None),
        P("section", "dp", None, None, None),
        P("section", "dp", None),
        P("section", None, "dp"),
        P("section", None),
        P("dp", None),
        P("dp", None),
        P("dp", None),
    )
    return jax.shard_map(
        body,
        mesh=mesh,
        in_specs=placed,
        out_specs=(
            P("section", "dp", None),
            P("section", "dp", None, None, None),
            P("section", "dp", None),
            P("section", None, "dp"),
            P("section", "dp"),
            P(None, ("dp", "section")),
        ),
        check_vma=False,
    )
```

```python
import functools

import jax
import jax.numpy as jnp
from jax import lax
from jax.experimental import pallas as pl
from jax.experimental.pallas import tpu as pltpu
from jax.sharding import PartitionSpec as P

SENT = 100
STREAMS = 2
TILES = 4
PAIR = 4
EPSILON = 1e-06


def layer_kernel(
    cross, start, number, active, *refs
):
    has_side = cross == "sided"
    grad, *refs = refs
    if has_side:
        side, *refs = refs
    (weights, probs_hbm, source_hbm, inverse_hbm, gain_hbm, _, _, _, _, _), refs = (
        refs[:10],
        refs[10:],
    )
    send, out_hbm, in_hbm, ctx_hbm, vgrad_hbm, term_hbm, *refs = refs
    probs, source, inverse, gain, ctx, vgrad, term, scaled, unit, sem = refs
    rows, width = grad.shape
    inner = ctx.shape[1]
    heads = probs.shape[0]
    head = inner // heads
    wide, tall = inner // TILES, width // TILES
    span = pl.ds(start * rows, rows)

    if number == 1:

        @pl.when(active[number] == 2)
        def _():
            copy = pltpu.make_async_copy(out_hbm.at[span], send, sem.at[10])
            copy.start()
            copy.wait()

    @pl.when(active[number] == 1)
    def _():
        loads = [
            pltpu.make_async_copy(origin, target, sem.at[index])
            for index, (origin, target) in enumerate(
                [
                    (probs_hbm.at[start], probs),
                    (source_hbm.at[span], source),
                    (inverse_hbm.at[span], inverse),
                    (gain_hbm, gain),
                ]
            )
        ]
        for load in loads:
            load.start()
        loads[0].wait()
        stores = [pltpu.make_async_copy(grad, out_hbm.at[span], sem.at[6])]
        if cross:
            stores.append(pltpu.make_async_copy(grad, in_hbm.at[span], sem.at[7]))
        for store in stores:
            store.start()
        arrived = grad[...]
        for tile in range(TILES):
            columns = slice(tile * wide, (tile + 1) * wide)
            piece = jnp.dot(
                arrived, weights[:, columns], preferred_element_type=jnp.float32
            ).astype(jnp.bfloat16)
            ctx[:, columns] = piece
            for index in range(wide // head):
                first = tile * wide + index * head
                vgrad[:, first : first + head] = jnp.dot(
                    probs[first // head],
                    piece[:, index * head : (index + 1) * head],
                    preferred_element_type=jnp.float32,
                ).astype(jnp.bfloat16)
        kept = [
            pltpu.make_async_copy(ctx, ctx_hbm.at[span], sem.at[8]),
            pltpu.make_async_copy(vgrad, vgrad_hbm.at[span], sem.at[9]),
        ]
        for store in kept:
            store.start()
        for load in loads[1:]:
            load.wait()
        value_grad = vgrad[...]
        scale = inverse[...]
        total = jnp.zeros((rows, 1), jnp.float32)
        for tile in range(TILES):
            columns = slice(tile * tall, (tile + 1) * tall)
            normed_grad = lax.dot_general(
                value_grad,
                weights[columns, inner:],
                (((1,), (1,)), ((), ())),
                preferred_element_type=jnp.float32,
            )
            unit_piece = source[:, columns].astype(jnp.float32) * scale
            product = normed_grad * unit_piece
            gain_piece = gain[:, columns]
            term[:, columns] = jnp.sum(product, axis=0, keepdims=True)
            total = total + jnp.sum(product * gain_piece, axis=1, keepdims=True)
            scaled[:, columns] = normed_grad * gain_piece
            unit[:, columns] = unit_piece
        source_grad = scale * (scaled[...] - unit[...] * (total / width))
        if has_side:
            source_grad = side[...].astype(jnp.float32) + source_grad
        elif not cross:
            source_grad = grad[...].astype(jnp.float32) + source_grad
        send[...] = source_grad.astype(jnp.bfloat16)
        last = [
            pltpu.make_async_copy(term, term_hbm.at[start], sem.at[11]),
        ]
        if not cross:
            last.append(pltpu.make_async_copy(send, in_hbm.at[span], sem.at[7]))
        for store in last:
            store.start()
        for store in stores + kept + last:
            store.wait()


def run_layer(cross, start, number, active, grad, side, fixed, stores):
    rows, width = grad.shape
    heads, inner = fixed[1].shape[1], stores[2].shape[1]
    far = pl.BlockSpec(memory_space=pltpu.HBM)
    near = pl.BlockSpec(memory_space=pltpu.VMEM)
    moving = [grad] + ([side] if cross == "sided" else [])
    shape = jax.ShapeDtypeStruct
    first = 1 + len(moving) + len(fixed)
    narrow = pltpu.VMEM((rows, width), jnp.bfloat16)
    inside = pltpu.VMEM((rows, inner), jnp.bfloat16)
    wide = pltpu.VMEM((rows, width), jnp.float32)
    send, *stores = pl.pallas_call(
        functools.partial(layer_kernel, cross, start, number),
        out_shape=(shape((rows, width), jnp.bfloat16),)
        + tuple(shape(store.shape, store.dtype) for store in stores),
        in_specs=[pl.BlockSpec(memory_space=pltpu.SMEM)]
        + [near] * (len(moving) + 1)
        + [far] * (len(fixed) - 1 + len(stores)),
        out_specs=(near,) + (far,) * len(stores),
        input_output_aliases={first + index: 1 + index for index in range(len(stores))},
        scratch_shapes=[
            pltpu.VMEM((heads, rows, rows), jnp.bfloat16),
            narrow,
            pltpu.VMEM((rows, 1), jnp.float32),
            pltpu.VMEM((1, width), jnp.float32),
            inside,
            inside,
            pltpu.VMEM((1, width), jnp.float32),
            wide,
            wide,
            pltpu.SemaphoreType.DMA((12,)),
        ],
        compiler_params=pltpu.CompilerParams(vmem_limit_bytes=20 * 1024 * 1024),
    )(active, *moving, *fixed, *stores)
    return send, tuple(stores)


def terms_kernel(normed, value_rows, out_rows, context, payload):
    pieces, rows, _ = payload.shape
    piece = rows // 2
    for index in range(pieces):
        columns = slice(index * piece, (index + 1) * piece)
        for first, left, right in ((0, normed, value_rows), (piece, out_rows, context)):
            payload[index, first : first + piece] = lax.dot_general(
                left[:, columns],
                right[...],
                (((0,), (0,)), ((), ())),
                preferred_element_type=jnp.float32,
            ).astype(payload.dtype)


def gradient_terms(normed, value_rows, out_rows, context, pieces):
    rows, width = normed.shape
    inner = context.shape[1]
    piece = width // pieces
    sliced = pl.BlockSpec((rows, PAIR * piece), lambda step: (0, step))
    whole = pl.BlockSpec((rows, inner), lambda step: (0, 0))
    return pl.pallas_call(
        terms_kernel,
        grid=(pieces // PAIR,),
        out_shape=pltpu.HBM((pieces, 2 * piece, inner), jnp.bfloat16),
        in_specs=[sliced, whole, sliced, whole],
        out_specs=pl.BlockSpec((PAIR, 2 * piece, inner), lambda step: (step, 0, 0)),
        compiler_params=pltpu.CompilerParams(vmem_limit_bytes=16 * 1024 * 1024),
    )(normed, value_rows, out_rows, context)


def body(
    section_inputs,
    enc_output,
    attention_probs,
    value_weight,
    out_weight,
    norm_gain,
    top_grad,
    enc_sentinel,
    dec_sentinel,
):
    count = lax.axis_size("section")
    dp_count = lax.axis_size("dp")
    half = count // 2
    section = lax.axis_index("section")
    in_decoder = section >= half
    is_cross = jnp.logical_and(in_decoder, (section - half) % 2 == 1)
    gathered = lax.all_gather(
        jnp.concatenate([out_weight[0].T, value_weight[0]], axis=1), "dp", axis=0, tiled=True
    )
    inner = value_weight.shape[2]
    w_value = gathered[:, inner:]
    gain_row = norm_gain[0]
    micro, length = enc_sentinel.shape
    width = section_inputs.shape[2]
    heads = attention_probs.shape[2]
    rows = micro * length
    group = micro // STREAMS
    block = group * length

    source = jnp.where(is_cross, enc_output, section_inputs[0])
    widened = source.astype(jnp.float32)
    inverse = lax.rsqrt(jnp.mean(widened * widened, axis=-1, keepdims=True) + EPSILON)
    normed = (widened * inverse * gain_row).astype(jnp.bfloat16)
    probs = attention_probs[0]
    blocks = probs.reshape(STREAMS, group, heads, length, length).transpose(0, 2, 1, 4, 3)
    spread = jnp.eye(group, dtype=probs.dtype)[None, None, :, None, :, None]
    diagonal = (blocks[:, :, :, :, None, :] * spread).reshape(STREAMS, heads, block, block)
    fixed = (gathered, diagonal, source, inverse, gain_row[None])
    stores = (
        jnp.zeros((rows, width), jnp.bfloat16),
        jnp.zeros((rows, width), jnp.bfloat16),
        jnp.zeros((rows, inner), jnp.bfloat16),
        jnp.zeros((rows, inner), jnp.bfloat16),
        jnp.zeros((STREAMS, 1, width), jnp.float32),
    )

    numbers = jnp.arange(count)
    active = jnp.where(section == numbers, 1, 0).astype(jnp.int32)
    active = jnp.where((section == half) & (numbers == 0), 1, active)
    active = jnp.where((section == half) & (numbers == half), 0, active)
    active = jnp.where((section == half + 1) & (numbers == 1), 2, active)

    def run(number, cross, start, grad, side, stores):
        with jax.named_scope(f"k{number}_{start}"):
            return run_layer(cross, start, number, active, grad, side, fixed, stores)

    def move(one, start, *pairs):
        with jax.named_scope(f"p{pairs[0][0]}_{pairs[0][1]}_{start}"):
            return lax.ppermute(one, "section", pairs)

    def after(one, other):
        return lax.optimization_barrier((one, other))[0]

    tops = [top_grad[start * block : (start + 1) * block] for start in range(STREAMS)]
    chosen = jnp.where(
        section == 0, enc_sentinel, jnp.where(section == half, dec_sentinel, SENT)
    )
    table = (chosen.reshape(1, -1) == jnp.arange(SENT, dtype=jnp.int32)[:, None]).astype(
        jnp.bfloat16
    )
    tops[0], table, active = lax.optimization_barrier((tops[0], table, active))
    main, side = [None] * STREAMS, [None] * STREAMS
    for start in range(STREAMS):
        main[start], stores = run(count - 2, "", start, tops[start], None, stores)
    grads = [move(main[start], start, (count - 2, count - 4)) for start in range(STREAMS)]
    grads[0] = after(grads[0], main[-1])
    given = [None] * STREAMS
    for number in range(count - 4, half, -2):
        target = number - 2 if number - 2 > half else half + 1
        relayed, following, sending = ([None] * STREAMS for _ in range(3))
        for start in range(STREAMS):
            grad = grads[start]
            if start:
                grad = after(grad, main[start - 1])
            relayed[start] = move(grad, start, (number, number + 1))
            if not start:
                grad = after(grad, relayed[start])
            main[start], stores = run(number, "", start, grad, None, stores)
            following[start] = move(main[start], start, (number, target))
            if number == count - 4:
                side[start], stores = run(count - 1, "open", start, tops[start], None, stores)
                given[start] = move(side[start], start, (count - 1, count - 3))
            one = relayed[start]
            if start and number > half + 2:
                one = after(one, sending[start - 1])
            side[start], stores = run(number + 1, "sided", start, one, given[start], stores)
            sending[start] = move(side[start], start, (number + 1, number - 1))
        grads, given = following, sending
        grads[0] = after(grads[0], main[-1])
    for number in [half + 1] + list(range(half - 1, -1, -1)):
        if number == half - 1:
            values = jnp.dot(after(normed, main[-1]), w_value, preferred_element_type=jnp.float32).astype(jnp.bfloat16)
            head_values = values.reshape(micro, length, heads, -1)
            context = jnp.einsum(
                "bhqk,bkhd->bqhd", probs, head_values, preferred_element_type=jnp.float32
            )
            context = context.astype(jnp.bfloat16).reshape(rows, inner)
        for start in range(STREAMS):
            if number == half - 1:
                pairs = [(half + 1, number)]
            elif number == 0:
                pairs = [(1, 0), (half + 1, half)]
            else:
                pairs = [(number + 1, number)]
            grad = grads[start] if number > half else move(main[start], start, *pairs)
            if start:
                grad = after(grad, main[start - 1])
            elif number == half - 1:
                grad, context, values = lax.optimization_barrier((grad, context, values))
            main[start], stores = run(
                number, "sided" if number > half else "", start, grad, given[start], stores
            )
    out_rows, in_rows, ctx_rows, value_rows, terms = stores
    gain_total = jnp.sum(terms, axis=(0, 1))
    head_grads = ctx_rows.reshape(micro, length, heads, -1)
    prob_grad = jnp.einsum(
        "bqhd,bkhd->bhqk", head_grads, head_values, preferred_element_type=jnp.float32
    )
    prob_wide = probs.astype(jnp.float32)
    score_grad = (
        prob_wide * (prob_grad - jnp.sum(prob_grad * prob_wide, axis=-1, keepdims=True))
    ).astype(jnp.bfloat16)
    piece = width // dp_count
    sentinel_term = jnp.dot(table, in_rows, preferred_element_type=jnp.float32)
    share = piece // count
    parts = sentinel_term.reshape(SENT, dp_count, count, share).transpose(2, 0, 1, 3)
    parts = parts.reshape(count, SENT, dp_count * share)
    parts = lax.all_to_all(parts, "section", 0, 0, tiled=True)
    payload = gradient_terms(normed, value_rows, out_rows, context, dp_count)
    summed = lax.psum_scatter(payload, "dp", scatter_dimension=0, tiled=True)[0]
    parts = (parts[0] + parts[half]).reshape(SENT, dp_count, share).transpose(1, 0, 2)
    parts = jnp.concatenate(
        [parts.reshape(dp_count, -1), gain_total.reshape(dp_count, piece)], axis=1
    )
    parts = jnp.pad(parts, ((0, 0), (0, -parts.shape[1] % 1024)))
    parts = parts.reshape(dp_count, -1, 128)
    parts = lax.all_to_all(parts, "dp", 0, 0, tiled=True)
    value_sum, output_sum = summed[:piece], summed[piece:].T
    parts, value_sum, output_sum = lax.optimization_barrier((parts, value_sum, output_sum))
    parts = jnp.sum(parts, axis=0).reshape(-1)
    sentinel_grad = parts[: SENT * share].reshape(SENT, share)
    gain_sum = parts[SENT * share : SENT * share + piece]
    return (
        in_rows[None],
        score_grad[None],
        value_sum[None],
        output_sum[None],
        gain_sum[None],
        sentinel_grad,
    )


def solution(mesh):
    placed = (
        P("section", "dp", None),
        P("dp", None),
        P("section", "dp", None, None, None),
        P("section", "dp", None),
        P("section", None, "dp"),
        P("section", None),
        P("dp", None),
        P("dp", None),
        P("dp", None),
    )
    return jax.shard_map(
        body,
        mesh=mesh,
        in_specs=placed,
        out_specs=(
            P("section", "dp", None),
            P("section", "dp", None, None, None),
            P("section", "dp", None),
            P("section", None, "dp"),
            P("section", "dp"),
            P(None, ("dp", "section")),
        ),
        check_vma=False,
    )
```
